512 devices in a mesh: row: 16 (over y, x), col: 32 (over z, core).
Axes of the slice: x: 4, y: 4, z: 16, core: 2. Of those that a mesh axis runs over, the one named last changes fastest.
Arguments:
- inputs: bfloat16 [1024, 6144], P('col', 'row'), may hold values from -6 to 6
- cotangent: bfloat16 [1024, 6144], P('col', 'row'), may hold values from -0.59765625 to 0.59765625
- weight_in: bfloat16 [6144, 24576], P('row', 'col'), may hold values from -0.078125 to 0.078125
- weight_out: bfloat16 [24576, 6144], P('col', 'row'), may hold values from -0.078125 to 0.078125
Outputs:
- grad_inputs: bfloat16 [1024, 6144], P('col', 'row')
- grad_weight_in: float32 [6144, 24576], P('row', 'col')
- grad_weight_out: float32 [24576, 6144], P('col', 'row')
The draws below stay inside these ranges and needn't reach their ends.
All inputs are finite; a program needn't handle non-finite values.
Results may differ from the reference program's by a relative error of at most 0.0049.
Values may be sent and summed in bfloat16 or wider, within the bound.
No kernel may reach another device: no remote copies, remote signals or barrier semaphores. Data moves between devices by JAX's collectives and lax.ppermute only.
A program may use at most 64 MiB of HBM per device.

```python
import jax
import jax.numpy as jnp
from jax import lax

D = 6144
F = 24576
TOKENS = 1024


def shard_levels(own_key, dims, cuts, smallest, largest):
    loudness = 1.0
    for position, shards_of in cuts:
        heights = jax.random.uniform(jax.random.fold_in(jax.random.fold_in(own_key, 6), position), (shards_of,), jnp.float32, smallest / len(cuts), largest / len(cuts))
        loudness = loudness * jnp.repeat(jnp.exp(heights), dims[position] // shards_of).reshape((-1,) + (1,) * (len(dims) - 1 - position))
    return loudness


def bell_draw(rng, extent, width, limit, cuts=(), kind=jnp.bfloat16):
    entries = width * jax.random.normal(rng, extent, jnp.float32)
    if cuts:
        entries = entries * shard_levels(rng, extent, cuts, -0.22, 0.18)
    return jnp.clip(entries, -limit, limit).astype(kind)


def setup_inputs(seed: int = 0) -> dict:
    keys = jax.random.split(jax.random.key(seed), 5)
    inputs = bell_draw(keys[0], (TOKENS, D), 1.0, 6.0, ((0, 32), (1, 16)))
    cotangent = bell_draw(keys[1], (TOKENS, D), 0.1, 0.59765625, ((0, 32), (1, 16)))
    weight_in = bell_draw(keys[2], (D, F), D ** -0.5, 0.078125, ((0, 16), (1, 32)))
    weight_out = bell_draw(keys[3], (F, D), D ** -0.5, 0.078125, ((0, 32), (1, 16)))
    return {"inputs": inputs, "cotangent": cotangent, "weight_in": weight_in, "weight_out": weight_out}


inv_sqrt_two = 0.7071067811865476
inv_sqrt_two_pi = 0.3989422804014327

def gelu_backward(preact, act_grad):
    normal_cdf = 0.5 * (1.0 + lax.erf(preact * inv_sqrt_two))
    normal_pdf = jnp.exp(-0.5 * preact * preact) * inv_sqrt_two_pi
    activated = (preact * normal_cdf).astype(jnp.bfloat16)
    pre_grad = (act_grad * (normal_cdf + preact * normal_pdf)).astype(jnp.bfloat16)
    return (activated, pre_grad)

def reference(inputs, cotangent, weight_in, weight_out):
    preact = jnp.dot(inputs, weight_in, preferred_element_type=jnp.float32)
    act_grad = jnp.dot(cotangent, weight_out.T, preferred_element_type=jnp.float32)
    activated, pre_grad = gelu_backward(preact, act_grad)
    grad_weight_out = jnp.dot(activated.T, cotangent, preferred_element_type=jnp.float32)
    grad_weight_in = jnp.dot(inputs.T, pre_grad, preferred_element_type=jnp.float32)
    grad_inputs = jnp.dot(pre_grad, weight_in.T, preferred_element_type=jnp.float32).astype(jnp.bfloat16)
    return (grad_inputs, grad_weight_in, grad_weight_out)
```

```python
import jax
import jax.numpy as jnp
import numpy as np
from jax import lax
from jax.sharding import Mesh
from jax.sharding import PartitionSpec as P

inv_sqrt_two = 0.7071067811865476
inv_sqrt_two_pi = 0.3989422804014327
ROW = ("y", "x")
COL = ("z", "core")
SWAP = [(0, 1), (1, 0)]


def gelu_backward(preact, act_grad):
    normal_cdf = 0.5 * (1.0 + lax.erf(preact * inv_sqrt_two))
    normal_pdf = jnp.exp(-0.5 * preact * preact) * inv_sqrt_two_pi
    activated = (preact * normal_cdf).astype(jnp.bfloat16)
    pre_grad = (act_grad * (normal_cdf + preact * normal_pdf)).astype(jnp.bfloat16)
    return (activated, pre_grad)


def dot(a, b, ca, cb):
    return lax.dot_general(a, b, (((ca,), (cb,)), ((), ())), preferred_element_type=jnp.float32)


def body(inputs, cotangent, weight_in, weight_out):
    rows, depth = inputs.shape
    hidden = weight_in.shape[1]
    n_row = lax.axis_size(ROW)
    n_z = lax.axis_size("z")
    both = jnp.stack([inputs, cotangent])
    own = lax.all_gather(both, "z", axis=1, tiled=True)
    other = lax.ppermute(own, "core", SWAP)
    full = jnp.concatenate([own, other], axis=1)
    x, g = full[0], full[1]
    tokens = x.shape[0]
    share = tokens // n_row
    pre_part = dot(x, weight_in, 1, 0).astype(jnp.bfloat16)
    grad_part = dot(g, weight_out, 1, 1).astype(jnp.bfloat16)
    parts = jnp.stack(
        [pre_part.reshape(n_row, share, hidden), grad_part.reshape(n_row, share, hidden)], axis=1
    )
    landed = lax.all_to_all(parts, ROW, 0, 0, tiled=True)
    sums = jnp.sum(landed.astype(jnp.float32), axis=0)
    activated, pre_grad = gelu_backward(sums[0], sums[1])
    hid = lax.all_gather(jnp.stack([activated, pre_grad]), ROW, axis=1, tiled=True)
    act, pg = hid[0], hid[1]
    gi = dot(pg, weight_in, 1, 1)
    half = tokens // 2
    mine = gi[:half] + lax.ppermute(gi[half:], "core", SWAP)
    pieces = lax.all_to_all(
        mine.astype(jnp.bfloat16).reshape(n_z, rows, depth), "z", 0, 0, tiled=True
    )
    grad_inputs = jnp.sum(pieces.astype(jnp.float32), axis=0).astype(jnp.bfloat16)
    grad_weight_out = dot(act, g, 0, 0)
    grad_weight_in = dot(x, pg, 0, 0)
    return (grad_inputs, grad_weight_in, grad_weight_out)


def solution(mesh):
    split = Mesh(mesh.devices.reshape(4, 4, 16, 2), ROW + COL)
    tok, w_in, w_out = P(COL, ROW), P(ROW, COL), P(COL, ROW)
    return jax.shard_map(
        body,
        mesh=split,
        in_specs=(tok, tok, w_in, w_out),
        out_specs=(tok, w_in, w_out),
        check_vma=False,
    )
```

```python
import jax
import jax.numpy as jnp
from jax import lax
from jax.sharding import Mesh
from jax.sharding import PartitionSpec as P

inv_sqrt_two = 0.7071067811865476
inv_sqrt_two_pi = 0.3989422804014327
ROW = ("y", "x")
COL = ("z", "core")
PLANE = ("y", "x", "core")
SWAP = [(0, 1), (1, 0)]
STEPS = (1, 3, 2)
NEAR = (0, 1, -1, 2)
FAR = (0, 4, -4, 8)


def gelu_backward(preact, act_grad):
    normal_cdf = 0.5 * (1.0 + lax.erf(preact * inv_sqrt_two))
    normal_pdf = jnp.exp(-0.5 * preact * preact) * inv_sqrt_two_pi
    activated = (preact * normal_cdf).astype(jnp.bfloat16)
    pre_grad = (act_grad * (normal_cdf + preact * normal_pdf)).astype(jnp.bfloat16)
    return (activated, pre_grad)


def dot(a, b, ca, cb):
    return lax.dot_general(a, b, (((ca,), (cb,)), ((), ())), preferred_element_type=jnp.float32)


def plane_hop(value, axis, step):
    pairs = []
    for y in range(4):
        for x in range(4):
            for core in range(2):
                if core == axis:
                    to = (y, (x + step) % 4)
                else:
                    to = ((y + step) % 4, x)
                pairs.append(((y * 4 + x) * 2 + core, (to[0] * 4 + to[1]) * 2 + core))
    return lax.ppermute(value, PLANE, pairs)


def z_hop(value, step):
    return lax.ppermute(value, "z", [(z, (z + step) % 16) for z in range(16)])


def turn(value, axis, by):
    return lax.dynamic_slice_in_dim(
        jnp.concatenate([value, value], axis=axis), by, value.shape[axis], axis
    )


def body(inputs, cotangent, weight_in, weight_out):
    rows, depth = inputs.shape
    hidden = weight_in.shape[1]
    core = lax.axis_index("core")
    pos_y, pos_x = lax.axis_index("y"), lax.axis_index("x")
    pos_a = jnp.where(core == 0, pos_x, pos_y)
    pos_b = jnp.where(core == 0, pos_y, pos_x)

    both = jnp.stack([inputs, cotangent])
    far = jnp.stack([both] + [z_hop(both, -step) for step in FAR[1:]], axis=1)
    own = jnp.stack([far] + [z_hop(far, -step) for step in NEAR[1:]], axis=1)
    other = lax.ppermute(own, "core", SWAP)
    full = jnp.stack([own, other], axis=1).reshape(2, 4, 4, -1, depth)
    full = turn(turn(full, 1, pos_a), 2, pos_b)
    tokens = full.shape[1] * full.shape[2] * full.shape[3]
    share = full.shape[3]
    x, g = full[0].reshape(tokens, depth), full[1].reshape(tokens, depth)

    pre_part = dot(x, weight_in, 1, 0).astype(jnp.bfloat16).reshape(4, 4 * share, hidden)
    grad_part = dot(g, weight_out, 1, 1).astype(jnp.bfloat16).reshape(4, 4 * share, hidden)
    parts = [jnp.stack([pre_part[d], grad_part[d]]) for d in range(4)]
    landed = [plane_hop(parts[d], 0, d) for d in STEPS]
    sums = parts[0].astype(jnp.float32) + sum(v.astype(jnp.float32) for v in landed)
    sums = sums.reshape(2, 4, share, hidden)
    sums = sums[:, 0] + sum(plane_hop(sums[:, d], 1, d) for d in STEPS)
    hid = jnp.stack(gelu_backward(sums[0], sums[1]))

    line = {0: hid}
    for d in STEPS:
        line[4 - d] = plane_hop(hid, 1, d)
    line = jnp.concatenate([line[d] for d in range(4)], axis=1)
    sheet = {0: line}
    for d in STEPS:
        sheet[4 - d] = plane_hop(line, 0, d)
    sheet = jnp.concatenate([sheet[d] for d in range(4)], axis=1)
    act, pg = sheet[0], sheet[1]

    gi = dot(pg, weight_in, 1, 1).reshape(4, 4, share, depth)
    gi = turn(turn(gi, 0, (4 - pos_a) % 4), 1, (4 - pos_b) % 4).reshape(2, 4, 4, rows, depth)
    chip = gi[0] + lax.ppermute(gi[1], "core", SWAP)
    near = chip.astype(jnp.bfloat16)
    near = chip[0] + sum(
        z_hop(near[j], NEAR[j]).astype(jnp.float32) for j in range(1, 4)
    )
    summed = near[0] + sum(z_hop(near[k], FAR[k]) for k in range(1, 4))
    grad_inputs = summed.astype(jnp.bfloat16)
    grad_weight_out = dot(act, g, 0, 0)
    grad_weight_in = dot(x, pg, 0, 0)
    return (grad_inputs, grad_weight_in, grad_weight_out)


def solution(mesh):
    split = Mesh(mesh.devices.reshape(4, 4, 16, 2), ROW + COL)
    tok, w_in, w_out = P(COL, ROW), P(ROW, COL), P(COL, ROW)
    return jax.shard_map(
        body,
        mesh=split,
        in_specs=(tok, tok, w_in, w_out),
        out_specs=(tok, w_in, w_out),
        check_vma=False,
    )
```

```python
import jax
import jax.numpy as jnp
from jax import lax
from jax.sharding import Mesh
from jax.sharding import PartitionSpec as P

inv_sqrt_two = 0.7071067811865476
inv_sqrt_two_pi = 0.3989422804014327
ROW = ("y", "x")
COL = ("z", "core")
PLANE = ("y", "x", "core")
SWAP = [(0, 1), (1, 0)]


def gelu_backward(preact, act_grad):
    normal_cdf = 0.5 * (1.0 + lax.erf(preact * inv_sqrt_two))
    normal_pdf = jnp.exp(-0.5 * preact * preact) * inv_sqrt_two_pi
    activated = (preact * normal_cdf).astype(jnp.bfloat16)
    pre_grad = (act_grad * (normal_cdf + preact * normal_pdf)).astype(jnp.bfloat16)
    return (activated, pre_grad)


def dot(a, b, ca, cb):
    return lax.dot_general(a, b, (((ca,), (cb,)), ((), ())), preferred_element_type=jnp.float32)


def device_in_plane(y, x, core):
    return (y * 4 + x) * 2 + core


def rings(axis):
    groups = []
    for core in range(2):
        for i in range(4):
            if core == axis:
                groups.append([device_in_plane(i, j, core) for j in range(4)])
            else:
                groups.append([device_in_plane(j, i, core) for j in range(4)])
    return groups


def swap_blocks(value, axis):
    return lax.all_to_all(value, PLANE, 0, 0, tiled=True, axis_index_groups=rings(axis))


def gather_ring(value, axis):
    return lax.all_gather(value, PLANE, axis=0, axis_index_groups=rings(axis))


def add_blocks(value):
    total = value[0].astype(jnp.float32)
    for i in range(1, value.shape[0]):
        total = total + value[i].astype(jnp.float32)
    return total


def gather_row(value):
    line = gather_ring(value, 1)
    sheet = swap_blocks(jnp.broadcast_to(line[None], (4,) + line.shape), 0)
    return sheet.reshape(-1, value.shape[-1])


def body(inputs, cotangent, weight_in, weight_out):
    rows, depth = inputs.shape
    hidden = weight_in.shape[1]
    own = lax.all_gather(jnp.stack([inputs, cotangent]), "z", axis=0)
    other = lax.ppermute(own, "core", SWAP)
    x = jnp.concatenate([own[:, 0], other[:, 0]]).reshape(-1, depth)
    g = jnp.concatenate([own[:, 1], other[:, 1]]).reshape(-1, depth)
    share = x.shape[0] // 16

    pre_part = dot(x, weight_in, 1, 0).astype(jnp.bfloat16).reshape(4, 4, share, hidden)
    grad_part = dot(g, weight_out, 1, 1).astype(jnp.bfloat16).reshape(4, 4, share, hidden)
    line = add_blocks(swap_blocks(jnp.stack([pre_part, grad_part], axis=2), 0))
    sums = add_blocks(swap_blocks(line, 1))
    activated, pre_grad = gelu_backward(sums[0], sums[1])

    pg = gather_row(pre_grad)
    gi = dot(pg, weight_in, 1, 1).reshape(2, 16, rows, depth)
    chip = gi[0] + lax.ppermute(gi[1], "core", SWAP)
    pieces, activated = lax.optimization_barrier((chip.astype(jnp.bfloat16), activated))
    pieces = lax.all_to_all(pieces, "z", 0, 0, tiled=True)
    act = gather_row(activated)
    grad_weight_in = dot(x, pg, 0, 0)
    grad_weight_out = dot(act, g, 0, 0)
    grad_inputs = add_blocks(pieces).astype(jnp.bfloat16)
    return (grad_inputs, grad_weight_in, grad_weight_out)


def solution(mesh):
    split = Mesh(mesh.devices.reshape(4, 4, 16, 2), ROW + COL)
    tok, w_in, w_out = P(COL, ROW), P(ROW, COL), P(COL, ROW)
    return jax.shard_map(
        body,
        mesh=split,
        in_specs=(tok, tok, w_in, w_out),
        out_specs=(tok, w_in, w_out),
        check_vma=False,
    )
```

```python
import jax
import jax.numpy as jnp
from jax import lax
from jax.sharding import Mesh
from jax.sharding import PartitionSpec as P

inv_sqrt_two = 0.7071067811865476
inv_sqrt_two_pi = 0.3989422804014327
ROW = ("y", "x")
COL = ("z", "core")
SWAP = [(0, 1), (1, 0)]


def gelu_backward(preact, act_grad):
    normal_cdf = 0.5 * (1.0 + lax.erf(preact * inv_sqrt_two))
    normal_pdf = jnp.exp(-0.5 * preact * preact) * inv_sqrt_two_pi
    activated = (preact * normal_cdf).astype(jnp.bfloat16)
    pre_grad = (act_grad * (normal_cdf + preact * normal_pdf)).astype(jnp.bfloat16)
    return (activated, pre_grad)


def dot(a, b, ca, cb):
    return lax.dot_general(a, b, (((ca,), (cb,)), ((), ())), preferred_element_type=jnp.float32)


def add_blocks(value):
    total = value[0].astype(jnp.float32)
    for i in range(1, value.shape[0]):
        total = total + value[i].astype(jnp.float32)
    return total


def body(inputs, cotangent, weight_in, weight_out):
    rows, depth = inputs.shape
    hidden = weight_in.shape[1]
    own = lax.all_gather(jnp.stack([inputs, cotangent]), "z", axis=0)
    other = lax.ppermute(own, "core", SWAP)
    x = jnp.concatenate([own[:, 0], other[:, 0]]).reshape(-1, depth)
    g = jnp.concatenate([own[:, 1], other[:, 1]]).reshape(-1, depth)
    share = x.shape[0] // 16

    pre_part = dot(x, weight_in, 1, 0)
    preact = lax.psum_scatter(pre_part, ROW, scatter_dimension=0, tiled=True)
    grad_part = dot(g, weight_out, 1, 1).astype(jnp.bfloat16).reshape(16, share, hidden)
    act_grad = add_blocks(lax.all_to_all(grad_part, ROW, 0, 0, tiled=True))
    activated, pre_grad = gelu_backward(preact, act_grad)

    act = lax.all_gather(activated, ROW, axis=0, tiled=True)
    copies = jnp.broadcast_to(pre_grad[None], (16, share, hidden))
    pg = lax.all_to_all(copies, ROW, 0, 0, tiled=True).reshape(-1, hidden)
    gi = dot(pg, weight_in, 1, 1).reshape(2, 16, rows, depth)
    chip = gi[0] + lax.ppermute(gi[1], "core", SWAP)
    pieces = lax.all_to_all(chip.astype(jnp.bfloat16), "z", 0, 0, tiled=True)
    grad_weight_in = dot(x, pg, 0, 0)
    grad_weight_out = dot(act, g, 0, 0)
    grad_inputs = add_blocks(pieces).astype(jnp.bfloat16)
    return (grad_inputs, grad_weight_in, grad_weight_out)


def solution(mesh):
    split = Mesh(mesh.devices.reshape(4, 4, 16, 2), ROW + COL)
    tok, w_in, w_out = P(COL, ROW), P(ROW, COL), P(COL, ROW)
    return jax.shard_map(
        body,
        mesh=split,
        in_specs=(tok, tok, w_in, w_out),
        out_specs=(tok, w_in, w_out),
        check_vma=False,
    )
```

```python
import jax
import jax.numpy as jnp
from jax import lax
from jax.sharding import Mesh
from jax.sharding import PartitionSpec as P

inv_sqrt_two = 0.7071067811865476
inv_sqrt_two_pi = 0.3989422804014327
ROW = ("y", "x")
COL = ("z", "core")
SWAP = [(0, 1), (1, 0)]


def normal_cdf(v):
    return 0.5 * (1.0 + lax.erf(v * inv_sqrt_two))


def normal_pdf(v):
    return jnp.exp(-0.5 * v * v) * inv_sqrt_two_pi


def dot(a, b, ca, cb):
    return lax.dot_general(a, b, (((ca,), (cb,)), ((), ())), preferred_element_type=jnp.float32)


def add_blocks(value):
    total = value[0].astype(jnp.float32)
    for i in range(1, value.shape[0]):
        total = total + value[i].astype(jnp.float32)
    return total


def gather_col(value):
    own = lax.all_gather(value, "z", axis=0, tiled=True)
    return jnp.concatenate([own, lax.ppermute(own, "core", SWAP)])


def sum_row(part):
    blocks = part.astype(jnp.bfloat16).reshape(16, -1, part.shape[-1])
    return add_blocks(lax.all_to_all(blocks, ROW, 0, 0, tiled=True))


def body(inputs, cotangent, weight_in, weight_out):
    rows, depth = inputs.shape
    hidden = weight_in.shape[1]
    x = gather_col(inputs)
    pre_part = dot(x, weight_in, 1, 0).astype(jnp.bfloat16)
    pre_part, cotangent = lax.optimization_barrier((pre_part, cotangent))
    preact = sum_row(pre_part)
    g = gather_col(cotangent)
    act_grad = sum_row(dot(g, weight_out, 1, 1))

    activated = (preact * normal_cdf(preact)).astype(jnp.bfloat16)
    act = lax.all_gather(activated, ROW, axis=0, tiled=True)
    pre_grad = (act_grad * (normal_cdf(preact) + preact * normal_pdf(preact))).astype(jnp.bfloat16)
    copies = jnp.broadcast_to(pre_grad[None], (16,) + pre_grad.shape)
    pg = lax.all_to_all(copies, ROW, 0, 0, tiled=True).reshape(-1, hidden)
    gi = dot(pg, weight_in, 1, 1).reshape(2, 16, rows, depth)
    chip = gi[0] + lax.ppermute(gi[1], "core", SWAP)
    pieces = lax.all_to_all(chip.astype(jnp.bfloat16), "z", 0, 0, tiled=True)
    grad_weight_in = dot(x, pg, 0, 0)
    grad_weight_out = dot(act, g, 0, 0)
    grad_inputs = add_blocks(pieces).astype(jnp.bfloat16)
    return (grad_inputs, grad_weight_in, grad_weight_out)


def solution(mesh):
    split = Mesh(mesh.devices.reshape(4, 4, 16, 2), ROW + COL)
    tok, w_in, w_out = P(COL, ROW), P(ROW, COL), P(COL, ROW)
    return jax.shard_map(
        body,
        mesh=split,
        in_specs=(tok, tok, w_in, w_out),
        out_specs=(tok, w_in, w_out),
        check_vma=False,
    )
```

```python
import jax
import jax.numpy as jnp
from jax import lax
from jax.sharding import Mesh
from jax.sharding import PartitionSpec as P

inv_sqrt_two = 0.7071067811865476
inv_sqrt_two_pi = 0.3989422804014327
ROW = ("y", "x")
COL = ("z", "core")
PLANE = ("y", "x", "core")
SWAP = [(0, 1), (1, 0)]


def normal_cdf(v):
    return 0.5 * (1.0 + lax.erf(v * inv_sqrt_two))


def normal_pdf(v):
    return jnp.exp(-0.5 * v * v) * inv_sqrt_two_pi


def dot(a, b, ca, cb):
    return lax.dot_general(a, b, (((ca,), (cb,)), ((), ())), preferred_element_type=jnp.float32)


def add_blocks(value):
    total = value[0].astype(jnp.float32)
    for i in range(1, value.shape[0]):
        total = total + value[i].astype(jnp.float32)
    return total


def rings(axis):
    groups = []
    for core in range(2):
        for i in range(4):
            if core == axis:
                groups.append([(i * 4 + j) * 2 + core for j in range(4)])
            else:
                groups.append([(j * 4 + i) * 2 + core for j in range(4)])
    return groups


def add_ring(blocks, axis):
    blocks = blocks.astype(jnp.bfloat16)
    return add_blocks(lax.all_to_all(blocks, PLANE, 0, 0, tiled=True, axis_index_groups=rings(axis)))


def body(inputs, cotangent, weight_in, weight_out):
    rows, depth = inputs.shape
    hidden = weight_in.shape[1]
    own = lax.all_gather(jnp.stack([inputs, cotangent]), "z", axis=0)
    other = lax.ppermute(own, "core", SWAP)
    x = jnp.concatenate([own[:, 0], other[:, 0]]).reshape(-1, depth)
    g = jnp.concatenate([own[:, 1], other[:, 1]]).reshape(-1, depth)
    share = x.shape[0] // 16

    def by_ring(value):
        sheet = value.reshape(4, 4, share, depth)
        turned = jnp.where(lax.axis_index("core") == 0, sheet.swapaxes(0, 1), sheet)
        return turned.reshape(-1, depth)

    pre_part = dot(by_ring(x), weight_in, 1, 0).astype(jnp.bfloat16).reshape(4, 4, share, hidden)
    grad_part = dot(by_ring(g), weight_out, 1, 1).astype(jnp.bfloat16).reshape(4, 4, share, hidden)
    sums = add_ring(add_ring(jnp.stack([pre_part, grad_part], axis=2), 0), 1)
    preact, act_grad = sums[0], sums[1]

    activated = (preact * normal_cdf(preact)).astype(jnp.bfloat16)
    act = lax.all_gather(activated, ROW, axis=0, tiled=True)
    pre_grad = (act_grad * (normal_cdf(preact) + preact * normal_pdf(preact))).astype(jnp.bfloat16)
    copies = jnp.broadcast_to(pre_grad[None], (16,) + pre_grad.shape)
    pg = lax.all_to_all(copies, ROW, 0, 0, tiled=True).reshape(-1, hidden)
    gi = dot(pg, weight_in, 1, 1).reshape(2, 16, rows, depth)
    chip = gi[0] + lax.ppermute(gi[1], "core", SWAP)
    pieces = lax.all_to_all(chip.astype(jnp.bfloat16), "z", 0, 0, tiled=True)
    grad_weight_in = dot(x, pg, 0, 0)
    grad_weight_out = dot(act, g, 0, 0)
    grad_inputs = add_blocks(pieces).astype(jnp.bfloat16)
    return (grad_inputs, grad_weight_in, grad_weight_out)


def solution(mesh):
    split = Mesh(mesh.devices.reshape(4, 4, 16, 2), ROW + COL)
    tok, w_in, w_out = P(COL, ROW), P(ROW, COL), P(COL, ROW)
    return jax.shard_map(
        body,
        mesh=split,
        in_specs=(tok, tok, w_in, w_out),
        out_specs=(tok, w_in, w_out),
        check_vma=False,
    )
```

```python
import jax
import jax.numpy as jnp
from jax import lax
from jax.sharding import Mesh
from jax.sharding import PartitionSpec as P

inv_sqrt_two = 0.7071067811865476
inv_sqrt_two_pi = 0.3989422804014327
ROW = ("y", "x")
COL = ("z", "core")
PLANE = ("y", "x", "core")
SWAP = [(0, 1), (1, 0)]


def normal_cdf(v):
    return 0.5 * (1.0 + lax.erf(v * inv_sqrt_two))


def normal_pdf(v):
    return jnp.exp(-0.5 * v * v) * inv_sqrt_two_pi


def dot(a, b, ca, cb):
    return lax.dot_general(a, b, (((ca,), (cb,)), ((), ())), preferred_element_type=jnp.float32)


def add_blocks(value):
    total = value[0].astype(jnp.float32)
    for i in range(1, value.shape[0]):
        total = total + value[i].astype(jnp.float32)
    return total


def rings(axis):
    groups = []
    for core in range(2):
        for i in range(4):
            if core == axis:
                groups.append([(i * 4 + j) * 2 + core for j in range(4)])
            else:
                groups.append([(j * 4 + i) * 2 + core for j in range(4)])
    return groups


def add_ring(blocks, own, pos, axis):
    landed = lax.all_to_all(blocks, PLANE, 0, 0, tiled=True, axis_index_groups=rings(axis))
    total = own
    for i in range(4):
        total = total + jnp.where(i == pos, 0.0, landed[i].astype(jnp.float32))
    return total


def hop(value, axis, step):
    pairs = []
    for ring in rings(axis):
        pairs += [(ring[i], ring[(i + step) % 4]) for i in range(4)]
    return lax.ppermute(value, PLANE, pairs)


def gather_from(value, axis):
    pieces = [value] + [hop(value, axis, 4 - step) for step in range(1, 4)]
    return jnp.concatenate(pieces)


def turn(value, axis, by):
    return lax.dynamic_slice_in_dim(
        jnp.concatenate([value, value], axis=axis), by, value.shape[axis], axis
    )


def body(inputs, cotangent, weight_in, weight_out):
    rows, depth = inputs.shape
    hidden = weight_in.shape[1]
    own = lax.all_gather(jnp.stack([inputs, cotangent]), "z", axis=0)
    other = lax.ppermute(own, "core", SWAP)
    x = jnp.concatenate([own[:, 0], other[:, 0]]).reshape(-1, depth)
    g = jnp.concatenate([own[:, 1], other[:, 1]]).reshape(-1, depth)
    share = x.shape[0] // 16

    first = lax.axis_index("core") == 0
    pos_y, pos_x = lax.axis_index("y"), lax.axis_index("x")
    pos_a, pos_b = jnp.where(first, pos_x, pos_y), jnp.where(first, pos_y, pos_x)

    def by_ring(value):
        sheet = value.reshape(4, 4, share, depth)
        return jnp.where(first, sheet.swapaxes(0, 1), sheet)

    x_ring, g_ring = by_ring(x), by_ring(g)
    flat = (-1, depth)
    pre_part = dot(x_ring.reshape(flat), weight_in, 1, 0).astype(jnp.bfloat16)
    grad_part = dot(g_ring.reshape(flat), weight_out, 1, 1).astype(jnp.bfloat16)
    parts = [part.reshape(4, 4, share, hidden) for part in (pre_part, grad_part)]
    own_x = lax.dynamic_index_in_dim(x_ring, pos_a, 0, keepdims=False).reshape(flat)
    own_g = lax.dynamic_index_in_dim(g_ring, pos_a, 0, keepdims=False).reshape(flat)
    own_parts = [dot(own_x, weight_in, 1, 0), dot(own_g, weight_out, 1, 1)]
    own_parts = [part.reshape(4, share, hidden) for part in own_parts]
    line = add_ring(jnp.stack(parts, axis=2), jnp.stack(own_parts, axis=1), pos_a, 0)
    own_line = lax.dynamic_index_in_dim(line, pos_b, 0, keepdims=False)
    sums = add_ring(line.astype(jnp.bfloat16), own_line, pos_b, 1)
    preact, act_grad = sums[0], sums[1]

    activated = (preact * normal_cdf(preact)).astype(jnp.bfloat16)
    act_line = gather_from(activated, 1)
    pre_grad = (act_grad * (normal_cdf(preact) + preact * normal_pdf(preact))).astype(jnp.bfloat16)
    copies = jnp.broadcast_to(pre_grad[None], (16,) + pre_grad.shape)
    pg = lax.all_to_all(copies, ROW, 0, 0, tiled=True).reshape(-1, hidden)
    pg, act_line = lax.optimization_barrier((pg, act_line))
    gi = dot(pg, weight_in, 1, 1).reshape(2, 16, rows, depth)
    chip = (gi[0] + lax.ppermute(gi[1], "core", SWAP)).astype(jnp.bfloat16)
    chip, pg = lax.optimization_barrier((chip, pg))
    pieces = lax.all_to_all(chip, "z", 0, 0, tiled=True)
    grad_weight_in = dot(x, pg, 0, 0)
    grad_weight_in, act_line = lax.optimization_barrier((grad_weight_in, act_line))
    act = gather_from(act_line, 0)
    g_from = turn(turn(g_ring, 0, pos_a), 1, pos_b).reshape(flat)
    grad_weight_out = dot(act, g_from, 0, 0)
    grad_inputs = add_blocks(pieces).astype(jnp.bfloat16)
    return (grad_inputs, grad_weight_in, grad_weight_out)


def solution(mesh):
    split = Mesh(mesh.devices.reshape(4, 4, 16, 2), ROW + COL)
    tok, w_in, w_out = P(COL, ROW), P(ROW, COL), P(COL, ROW)
    return jax.shard_map(
        body,
        mesh=split,
        in_specs=(tok, tok, w_in, w_out),
        out_specs=(tok, w_in, w_out),
        check_vma=False,
    )
```

```python
import jax
import jax.numpy as jnp
from jax import lax
from jax.sharding import Mesh
from jax.sharding import PartitionSpec as P

inv_sqrt_two = 0.7071067811865476
inv_sqrt_two_pi = 0.3989422804014327
ROW = ("y", "x")
COL = ("z", "core")
PLANE = ("y", "x", "core")
SWAP = [(0, 1), (1, 0)]


def normal_cdf(v):
    return 0.5 * (1.0 + lax.erf(v * inv_sqrt_two))


def normal_pdf(v):
    return jnp.exp(-0.5 * v * v) * inv_sqrt_two_pi


def dot(a, b, ca, cb):
    return lax.dot_general(a, b, (((ca,), (cb,)), ((), ())), preferred_element_type=jnp.float32)


def add_blocks(value):
    total = value[0].astype(jnp.float32)
    for i in range(1, value.shape[0]):
        total = total + value[i].astype(jnp.float32)
    return total


def rings(axis):
    groups = []
    for core in range(2):
        for i in range(4):
            if core == axis:
                groups.append([(i * 4 + j) * 2 + core for j in range(4)])
            else:
                groups.append([(j * 4 + i) * 2 + core for j in range(4)])
    return groups


def swap_ring(blocks, axis):
    return lax.all_to_all(blocks, PLANE, 0, 0, tiled=True, axis_index_groups=rings(axis))


def hop(value, axis, step):
    pairs = []
    for ring in rings(axis):
        pairs += [(ring[i], ring[(i + step) % 4]) for i in range(4)]
    return lax.ppermute(value, PLANE, pairs)


def gather_from(value, axis):
    pieces = [value] + [hop(value, axis, 4 - step) for step in range(1, 4)]
    return jnp.concatenate(pieces)


def turn(value, axis, by):
    return lax.dynamic_slice_in_dim(
        jnp.concatenate([value, value], axis=axis), by, value.shape[axis], axis
    )


def body(inputs, cotangent, weight_in, weight_out):
    rows, depth = inputs.shape
    hidden = weight_in.shape[1]
    own = lax.all_gather(jnp.stack([inputs, cotangent]), "z", axis=0)
    other = lax.ppermute(own, "core", SWAP)
    x = jnp.concatenate([own[:, 0], other[:, 0]]).reshape(-1, depth)
    g = jnp.concatenate([own[:, 1], other[:, 1]]).reshape(-1, depth)
    share = x.shape[0] // 16

    first = lax.axis_index("core") == 0
    pos_y, pos_x = lax.axis_index("y"), lax.axis_index("x")
    pos_a, pos_b = jnp.where(first, pos_x, pos_y), jnp.where(first, pos_y, pos_x)

    def by_ring(value):
        sheet = value.reshape(4, 4, share, depth)
        return jnp.where(first, sheet.swapaxes(0, 1), sheet)

    x_ring, g_ring = by_ring(x), by_ring(g)
    flat = (-1, depth)
    pre_part = dot(x_ring.reshape(flat), weight_in, 1, 0).astype(jnp.bfloat16)
    grad_part = dot(g_ring.reshape(flat), weight_out, 1, 1).astype(jnp.bfloat16)
    parts = [part.reshape(4, 4, share, hidden) for part in (pre_part, grad_part)]
    line = add_blocks(swap_ring(jnp.stack(parts, axis=2), 0))
    sums = lax.dynamic_index_in_dim(line, pos_b, 0, keepdims=False)
    landed = swap_ring(line.astype(jnp.bfloat16), 1)
    for i in range(4):
        sums = sums + jnp.where(i == pos_b, 0.0, landed[i].astype(jnp.float32))
    preact, act_grad = sums[0], sums[1]

    activated = (preact * normal_cdf(preact)).astype(jnp.bfloat16)
    act_line = gather_from(activated, 1)
    pre_grad = (act_grad * (normal_cdf(preact) + preact * normal_pdf(preact))).astype(jnp.bfloat16)
    copies = jnp.broadcast_to(pre_grad[None], (16,) + pre_grad.shape)
    pg = lax.all_to_all(copies, ROW, 0, 0, tiled=True).reshape(-1, hidden)
    pg, act_line = lax.optimization_barrier((pg, act_line))
    gi = dot(pg, weight_in, 1, 1).reshape(2, 16, rows, depth)
    chip = (gi[0] + lax.ppermute(gi[1], "core", SWAP)).astype(jnp.bfloat16)
    chip, pg = lax.optimization_barrier((chip, pg))
    pieces = lax.all_to_all(chip, "z", 0, 0, tiled=True)
    grad_weight_in = dot(x, pg, 0, 0)
    grad_weight_in, act_line = lax.optimization_barrier((grad_weight_in, act_line))
    act = gather_from(act_line, 0)
    g_from = turn(turn(g_ring, 0, pos_a), 1, pos_b).reshape(flat)
    grad_weight_out = dot(act, g_from, 0, 0)
    grad_inputs = add_blocks(pieces).astype(jnp.bfloat16)
    return (grad_inputs, grad_weight_in, grad_weight_out)


def solution(mesh):
    split = Mesh(mesh.devices.reshape(4, 4, 16, 2), ROW + COL)
    tok, w_in, w_out = P(COL, ROW), P(ROW, COL), P(COL, ROW)
    return jax.shard_map(
        body,
        mesh=split,
        in_specs=(tok, tok, w_in, w_out),
        out_specs=(tok, w_in, w_out),
        check_vma=False,
    )
```
